768 devices in a mesh: replica: 96 (over y_hi, z, core), fsdp: 8 (over x, y_lo).
Axes of the slice: x: 4, y: 8 (y_hi: 4, y_lo: 2; y = y_hi * 2 + y_lo), z: 12, core: 2. Of those that a mesh axis runs over, the one named last changes fastest.
Arguments:
- pseudo_grad: bfloat16 [96, 8192, 512], P('replica', 'fsdp'), may hold values from -448 to 448
- block_exponent: int32 [96, 8192, 4], P('replica', 'fsdp'), may hold values from -10 to -6
- base_params: bfloat16 [8192, 512], P('fsdp'), may hold values from -0.29882812 to 0.29882812
- outer_momentum: float32 [8192, 512], P('fsdp'), may hold values from -0.3 to 0.3
- tokens: bfloat16 [98304, 8192], P(('replica', 'fsdp')), may hold values from -6 to 6
- norm_gain: bfloat16 [8192], replicated, may hold values from 0.5 to 1.5
- kv_weight: bfloat16 [2, 8192, 512], P(None, 'fsdp'), may hold values from -0.0625 to 0.0625
Outputs:
- new_params: bfloat16 [8192, 512], P('fsdp')
- new_momentum: float32 [8192, 512], P('fsdp')
- keys_values: bfloat16 [98304, 1024], P(('replica', 'fsdp'))
The draws below stay inside these ranges and needn't reach their ends.
All inputs are finite; a program needn't handle non-finite values.
Results may differ from the reference program's by a relative error of at most 0.0049.
Values may be sent and summed in bfloat16 or wider, within the bound.
No kernel may reach another device: no remote copies, remote signals or barrier semaphores. Data moves between devices by JAX's collectives and lax.ppermute only.
A program may use at most 128 MiB of HBM per device.

```python
import jax
import jax.numpy as jnp
from jax import lax

D = 8192
HW = 512
BLOCK = 128
TOK_DEV = 128
REPLICAS = 96
TOKENS = 98304


def plant(values, rng, smallest, largest):
    shape = values.shape
    place = [jax.random.randint(jax.random.fold_in(rng, axis), (), 0, shape[axis]) for axis in range(len(shape))]
    values = values.at[tuple(place)].set(smallest)
    longest = shape.index(max(shape))
    place[longest] = (place[longest] + 1) % shape[longest]
    return values.at[tuple(place)].set(largest)


def level_of(own_key, shape, cuts, smallest, largest):
    gain, own = 1.0, jax.random.fold_in(own_key, 6)
    for position, parts in cuts:
        heights = jnp.exp(jax.random.uniform(jax.random.fold_in(own, position), (parts,), jnp.float32, smallest / len(cuts), largest / len(cuts)))
        gain = gain * jnp.repeat(heights, shape[position] // parts).reshape([-1 if axis == position else 1 for axis in range(len(shape))])
    return gain


def scatter_about(key, dims, scale, limit, cuts=(), dtype=jnp.bfloat16):
    entries = scale * jax.random.normal(key, dims, jnp.float32)
    if cuts:
        entries = entries * level_of(key, dims, cuts, -0.22, 0.18)
    return jnp.clip(entries, -limit, limit).astype(dtype)


def setup_inputs(seed: int = 0) -> dict:
    seeds = jax.random.split(jax.random.key(seed), 8)
    pseudo_grad = scatter_about(seeds[0], (REPLICAS, D, HW), 64.0, 448.0, ((0, 96), (1, 8)))
    block_exponent = plant(jax.random.randint(seeds[1], (REPLICAS, D, HW // BLOCK), -10, -5), jax.random.fold_in(seeds[1], 1), -10, (-5) - 1).astype(jnp.int32)
    base_params = scatter_about(seeds[2], (D, HW), 0.05, 0.29882812, ((0, 8),))
    outer_momentum = scatter_about(seeds[3], (D, HW), 0.05, 0.3, ((0, 8),), jnp.float32)
    tokens = scatter_about(seeds[4], (TOKENS, D), 1.0, 6.0, ((0, 768),))
    norm_gain = jnp.clip(1.0 + 0.1 * jax.random.normal(seeds[5], (D,), jnp.float32), 0.5, 1.5).astype(jnp.bfloat16)
    kv_weight = scatter_about(seeds[6], (2, D, HW), D ** -0.5, 0.0625, ((1, 8),))
    return {"pseudo_grad": pseudo_grad, "block_exponent": block_exponent, "base_params": base_params, "outer_momentum": outer_momentum, "tokens": tokens, "norm_gain": norm_gain, "kv_weight": kv_weight}


outer_rate = 0.7
momentum_coef = 0.9

def dequantize(values, exponents):
    rows = values.shape[0]
    blocks = exponents.shape[1]
    scale = jnp.exp2(exponents.astype(jnp.float32))
    shaped = values.astype(jnp.float32).reshape(rows, blocks, -1) * scale[:, :, None]
    return shaped.reshape(rows, -1)

def reference(pseudo_grad, block_exponent, base_params, outer_momentum, tokens, norm_gain, kv_weight):

    def accumulate(total, pair):
        return (total + dequantize(pair[0], pair[1]), None)
    start = jnp.zeros(base_params.shape, jnp.float32)
    total, unused = lax.scan(accumulate, start, (pseudo_grad, block_exponent))
    average = total / REPLICAS
    new_momentum = momentum_coef * outer_momentum + average
    new_params = (base_params.astype(jnp.float32) - outer_rate * (average + momentum_coef * new_momentum)).astype(jnp.bfloat16)
    weight_whole = kv_weight.astype(jnp.float32)
    gain_whole = norm_gain.astype(jnp.float32)

    def project(block):
        wide = block.astype(jnp.float32)
        meansq = lax.optimization_barrier(jnp.mean(wide * wide, axis=-1, keepdims=True))
        normed = (wide * lax.rsqrt(meansq + 1e-05) * gain_whole).astype(jnp.bfloat16)
        result = jnp.einsum('tn,knh->tkh', normed.astype(jnp.float32), weight_whole)
        return result.reshape(block.shape[0], -1).astype(jnp.bfloat16)
    grouped = tokens.reshape(-1, TOK_DEV, D)
    keys_values = lax.map(project, grouped).reshape(TOKENS, 2 * HW)
    return (new_params, new_momentum, keys_values)
```

```python
import functools

import jax
import jax.numpy as jnp
from jax import lax
from jax.experimental import pallas as pl
from jax.experimental.pallas import tpu as pltpu
from jax.sharding import Mesh
from jax.sharding import PartitionSpec as P

outer_rate = 0.7
momentum_coef = 0.9
f32, bf16 = jnp.float32, jnp.bfloat16
VMEM_LIMIT = 48 * 1024 * 1024

SHAPE = (4, 3, 4, 2, 4, 2)
NAMES = ("yh", "zh", "zl", "core", "x", "yl")
REPLICA = ("yh", "zh", "zl", "core")
FSDP = ("x", "yl")
GROUP = ("yh", "zl")


def vmem():
    return pl.BlockSpec(memory_space=pltpu.VMEM)


def smem():
    return pl.BlockSpec(memory_space=pltpu.SMEM)


def params():
    return pltpu.CompilerParams(vmem_limit_bytes=VMEM_LIMIT)


def shift(value, axis, by):
    n = lax.axis_size(axis)
    return lax.ppermute(value, axis, [(i, (i + by) % n) for i in range(n)])


def dequantize_kernel(place, values, exponents, keep, send):
    half, width = keep.shape
    blocks = exponents.shape[0]
    core = place[2]
    scale = jnp.exp2(exponents[...].astype(f32))
    lane = lax.broadcasted_iota(jnp.int32, (blocks, width), 1)
    row = lax.broadcasted_iota(jnp.int32, (blocks, width), 0)
    spread = jnp.where(lane // (width // blocks) == row, 1.0, 0.0).astype(f32)
    for out, part in ((keep, core), (send, 1 - core)):
        start = pl.multiple_of(part * half, half)
        mine = jnp.where(part == 0, scale[:, :half], scale[:, half:])
        wide = lax.dot_general(
            mine.astype(bf16),
            spread.astype(bf16),
            (((0,), (0,)), ((), ())),
            preferred_element_type=f32,
        )
        out[...] = (values[pl.ds(start, half), :].astype(f32) * wide).astype(bf16)


def dequantize(place, values, exponents):
    rows, width = values.shape
    half = jax.ShapeDtypeStruct((rows // 2, width), bf16)
    return pl.pallas_call(
        dequantize_kernel,
        out_shape=(half, half),
        in_specs=[smem(), vmem(), vmem()],
        out_specs=(vmem(), vmem()),
        compiler_params=params(),
        cost_estimate=pl.CostEstimate(
            flops=4 * rows * width, bytes_accessed=4 * rows * width, transcendentals=0
        ),
        name="dequantize",
    )(place, values, exponents)


def update_kernel(place, own, other, base, momentum, new_params, new_momentum):
    step = pl.program_id(0)
    steps = pl.num_programs(0)

    def run(average):
        average = average.astype(f32)
        fresh = momentum_coef * momentum[...] + average
        new_momentum[...] = fresh
        new_params[...] = (
            base[...].astype(f32) - outer_rate * (average + momentum_coef * fresh)
        ).astype(bf16)

    @pl.when(step < steps // 2)
    def _():
        run(own[...])

    @pl.when(step >= steps // 2)
    def _():
        run(other[...])


def update(place, own, other, base, momentum):
    rows, width = base.shape
    steps = 4
    each = rows // steps
    near = steps // 2

    def row(i, place):
        return (lax.rem(i + place[2] * near, steps), 0)

    return pl.pallas_call(
        update_kernel,
        out_shape=(
            jax.ShapeDtypeStruct((rows, width), bf16),
            jax.ShapeDtypeStruct((rows, width), f32),
        ),
        grid_spec=pltpu.PrefetchScalarGridSpec(
            num_scalar_prefetch=1,
            grid=(steps,),
            in_specs=[
                pl.BlockSpec((each, width), lambda i, place: (jnp.minimum(i, near - 1), 0)),
                pl.BlockSpec((each, width), lambda i, place: (jnp.maximum(i - near, 0), 0)),
                pl.BlockSpec((each, width), row),
                pl.BlockSpec((each, width), row),
            ],
            out_specs=[pl.BlockSpec((each, width), row), pl.BlockSpec((each, width), row)],
        ),
        compiler_params=params(),
        cost_estimate=pl.CostEstimate(
            flops=8 * rows * width, bytes_accessed=14 * rows * width, transcendentals=0
        ),
        name="update",
    )(place, own, other, base, momentum)


def gather_group(value):
    group = lax.axis_size(GROUP)
    value = lax.all_to_all(
        jnp.broadcast_to(value, (group, *value.shape)), GROUP, 0, 0, tiled=True
    )
    return value.reshape(-1, value.shape[-1])


def scatter_group(value):
    group = lax.axis_size(GROUP)
    parts = value.reshape(group, value.shape[0] // group, value.shape[1])
    parts = lax.all_to_all(parts, GROUP, 0, 0, tiled=True)
    return jnp.sum(parts.astype(f32), axis=0)


def sum_thirds(value):
    third = lax.axis_size("zh")
    whole = lax.all_to_all(
        jnp.broadcast_to(value, (third, *value.shape)), "zh", 0, 0, tiled=True
    )
    return jnp.sum(whole, axis=0)


def norm_kernel(place, tokens, gain, weight, *refs):
    outs, share, done = refs[:-2], refs[-2], refs[-1]
    x, yl, core = place[0], place[1], place[2]
    rows = share.shape[1]
    copy = pltpu.make_async_copy(
        weight.at[:, pl.ds(pl.multiple_of(core * rows, rows), rows), :], share, done
    )
    copy.start()
    peers = len(outs)
    width = tokens.shape[1]
    block = width // peers
    half, quarter = block // 2, block // 4
    total = jnp.zeros((tokens.shape[0], 128), f32)
    for at in range(0, width, 128):
        piece = tokens[:, at : at + 128].astype(f32)
        total += piece * piece
    meansq = jnp.sum(total, axis=1, keepdims=True) / width
    scale = lax.rsqrt(meansq + 1e-05)
    for k, out in enumerate(outs):
        first = lax.rem(x + k, peers) * block
        for at, start, size in (
            (0, yl * half, half),
            (half, (1 - yl) * half + core * quarter, quarter),
            (half + quarter, (1 - yl) * half + (1 - core) * quarter, quarter),
        ):
            columns = pl.ds(pl.multiple_of(first + start, quarter), size)
            piece = tokens[:, columns].astype(f32) * scale * gain[:, columns].astype(f32)
            out[:, at : at + size] = piece.astype(bf16)
    copy.wait()


def normalize(place, tokens, gain, weight):
    rows, width = tokens.shape
    peers = lax.axis_size("x")
    kinds, depth, columns = weight.shape
    hbm = pl.BlockSpec(memory_space=pl.ANY)
    return pl.pallas_call(
        norm_kernel,
        out_shape=(jax.ShapeDtypeStruct((rows, width // peers), bf16),) * peers
        + (jax.ShapeDtypeStruct((kinds, depth // 2, columns), bf16),),
        in_specs=[smem(), vmem(), vmem(), hbm],
        out_specs=(vmem(),) * peers + (hbm,),
        scratch_shapes=[pltpu.SemaphoreType.DMA],
        compiler_params=params(),
        cost_estimate=pl.CostEstimate(
            flops=6 * rows * width, bytes_accessed=4 * rows * width, transcendentals=0
        ),
        name="normalize",
    )(place, tokens, gain, weight)


def project_kernel(*refs):
    n = (len(refs) - 3) // 2
    tokens, (mine, near, far), outs = refs[:n], refs[n : n + 3], refs[n + 3 :]
    half, quarter, width = mine.shape[1], near.shape[1], mine.shape[2]
    for block, out in zip(tokens, outs, strict=True):
        for k in range(mine.shape[0]):
            total = jnp.dot(block[:, :half], mine[k], preferred_element_type=f32)
            total += jnp.dot(
                block[:, half : half + quarter], near[k], preferred_element_type=f32
            )
            total += jnp.dot(block[:, half + quarter :], far[k], preferred_element_type=f32)
            out[:, k * width : (k + 1) * width] = total.astype(out.dtype)


def project(tokens, weights):
    rows, depth = tokens[0].shape
    width = weights[0].shape[0] * weights[0].shape[2]
    n = len(tokens)
    return pl.pallas_call(
        project_kernel,
        out_shape=(jax.ShapeDtypeStruct((rows, width), f32),)
        + (jax.ShapeDtypeStruct((rows, width), bf16),) * (n - 1),
        in_specs=[vmem()] * (n + 3),
        out_specs=(vmem(),) * n,
        compiler_params=params(),
        cost_estimate=pl.CostEstimate(
            flops=2 * n * rows * depth * width,
            bytes_accessed=2 * depth * width + 2 * n * rows * depth + 4 * n * rows * width,
            transcendentals=0,
        ),
        name="project",
    )(*tokens, *weights)


def neighbour_share(share):
    yh, cores, yl = (lax.axis_size(a) for a in ("yh", "core", "yl"))
    ys = yh * yl
    moves = []
    for y in range(ys):
        for core in range(cores):
            to = (y + (1 if core == 0 else -1)) % ys
            moves.append(tuple((v // yl * cores + core) * yl + v % yl for v in (y, to)))
    return lax.ppermute(share, ("yh", "core", "yl"), moves)


def body(pseudo_grad, block_exponent, base_params, outer_momentum, tokens, norm_gain, kv_weight):
    x, yl, core = (lax.axis_index(a) for a in ("x", "yl", "core"))
    place = jnp.stack([x, yl, core]).astype(jnp.int32)
    after = lax.optimization_barrier

    keep, send = dequantize(place, pseudo_grad[0], block_exponent[0].T)
    got = shift(send, "core", 1)

    (tokens, _) = after((tokens, send))
    *blocks, share = normalize(place, tokens, norm_gain.reshape(1, -1), kv_weight)
    arrived = [blocks[0]] + [shift(block, "x", k) for k, block in enumerate(blocks) if k]
    near = neighbour_share(share)

    pair = (keep.astype(f32) + got.astype(f32)).astype(bf16)
    total = scatter_group(pair)
    total, near, *arrived = after((total, near, *arrived))
    far = shift(near, "core", 1)
    average = (sum_thirds(total) / lax.axis_size(REPLICA)).astype(bf16)

    partial = project(arrived, (kv_weight, near, far))
    average, *partial = after((average, *partial))
    average = gather_group(average)
    other = shift(average, "core", 1)

    total = partial[0]
    for k, part in enumerate(partial):
        if k:
            total = total + shift(part, "x", -k).astype(f32)
    keys_values = total.astype(bf16)

    new_params, new_momentum = update(place, average, other, base_params, outer_momentum)
    return (new_params, new_momentum, keys_values)


def solution(mesh):
    cut = Mesh(mesh.devices.reshape(SHAPE), NAMES)
    placed = (
        P(REPLICA, FSDP, None),
        P(REPLICA, FSDP, None),
        P(FSDP, None),
        P(FSDP, None),
        P((*REPLICA, *FSDP), None),
        P(),
        P(None, FSDP, None),
    )
    return jax.shard_map(
        body,
        mesh=cut,
        in_specs=placed,
        out_specs=(P(FSDP, None), P(FSDP, None), P((*REPLICA, *FSDP), None)),
        check_vma=False,
    )
```

```python
import functools

import jax
import jax.numpy as jnp
from jax import lax
from jax.experimental import pallas as pl
from jax.experimental.pallas import tpu as pltpu
from jax.sharding import Mesh
from jax.sharding import PartitionSpec as P

outer_rate = 0.7
momentum_coef = 0.9
f32, bf16 = jnp.float32, jnp.bfloat16
VMEM_LIMIT = 48 * 1024 * 1024

SHAPE = (4, 3, 4, 2, 4, 2)
NAMES = ("yh", "zh", "zl", "core", "x", "yl")
REPLICA = ("yh", "zh", "zl", "core")
FSDP = ("x", "yl")
GROUP = ("yh", "zl")


def vmem():
    return pl.BlockSpec(memory_space=pltpu.VMEM)


def smem():
    return pl.BlockSpec(memory_space=pltpu.SMEM)


def params():
    return pltpu.CompilerParams(vmem_limit_bytes=VMEM_LIMIT)


def shift(value, axis, by):
    n = lax.axis_size(axis)
    return lax.ppermute(value, axis, [(i, (i + by) % n) for i in range(n)])


def hbm():
    return pl.BlockSpec(memory_space=pl.ANY)


def front_kernel(place, gain, exponents, tokens, values, weight, *refs):
    (*blocks, keep, send, share), scratch = refs[: -len(FRONT)], refs[-len(FRONT) :]
    x, yl, core = place[0], place[1], place[2]
    held, normed, delta, dequantized, token_in, block_out, delta_in, delta_out, moved = scratch
    peers, rows, block = normed.shape
    half, quarter = block // 2, block // 4

    def chunk(i):
        at = pl.ds(i * block, block)
        return pltpu.make_async_copy(tokens.at[:, at], held.at[:, at], token_in.at[i])

    for i in range(peers):
        chunk(i).start()
    delta_copy = pltpu.make_async_copy(values, delta, delta_in)
    delta_copy.start()
    depth = share.shape[1]
    mine = pl.ds(pl.multiple_of(core * depth, depth), depth)
    share_copy = pltpu.make_async_copy(weight.at[:, mine, :], share, moved)
    share_copy.start()

    total = jnp.zeros((rows, 128), f32)
    for i in range(peers):
        chunk(i).wait()
        for at in range(i * block, (i + 1) * block, 128):
            piece = held[:, at : at + 128].astype(f32)
            total += piece * piece
    meansq = jnp.sum(total, axis=1, keepdims=True) / (peers * block)
    scale = lax.rsqrt(meansq + 1e-05)
    outs = []
    for k in (*range(1, peers), 0):
        first = lax.rem(x + k, peers) * block
        for at, start, size in (
            (0, yl * half, half),
            (half, (1 - yl) * half + core * quarter, quarter),
            (half + quarter, (1 - yl) * half + (1 - core) * quarter, quarter),
        ):
            columns = pl.ds(pl.multiple_of(first + start, quarter), size)
            piece = held[:, columns].astype(f32) * scale * gain[:, columns].astype(f32)
            normed[k, :, at : at + size] = piece.astype(bf16)
        outs.append(pltpu.make_async_copy(normed.at[k], blocks[k], block_out.at[k]))
        outs[-1].start()

    near, width = keep.shape
    count = exponents.shape[0]
    power = jnp.exp2(exponents[...].astype(f32))
    lane = lax.broadcasted_iota(jnp.int32, (count, width), 1)
    row = lax.broadcasted_iota(jnp.int32, (count, width), 0)
    spread = jnp.where(lane // (width // count) == row, 1.0, 0.0).astype(bf16)
    delta_copy.wait()
    for i, (out, part) in enumerate(((send, 1 - core), (keep, core))):
        start = pl.multiple_of(part * near, near)
        own = jnp.where(part == 0, power[:, :near], power[:, near:]).astype(bf16)
        wide = lax.dot_general(own, spread, (((0,), (0,)), ((), ())), preferred_element_type=f32)
        dequantized[i] = (delta[pl.ds(start, near), :].astype(f32) * wide).astype(bf16)
        outs.append(pltpu.make_async_copy(dequantized.at[i], out, delta_out.at[i]))
        outs[-1].start()
    for copy in (*outs, share_copy):
        copy.wait()


FRONT = ("held", "normed", "delta", "dequantized", "in", "out", "din", "dout", "moved")


def front(place, tokens, gain, values, exponents, weight):
    rows, width = tokens.shape
    peers = lax.axis_size("x")
    block = width // peers
    deep, across = values.shape
    kinds, depth, columns = weight.shape
    dma = pltpu.SemaphoreType.DMA
    return pl.pallas_call(
        front_kernel,
        out_shape=(jax.ShapeDtypeStruct((rows, block), bf16),) * peers
        + (jax.ShapeDtypeStruct((deep // 2, across), bf16),) * 2
        + (jax.ShapeDtypeStruct((kinds, depth // 2, columns), bf16),),
        in_specs=[smem(), vmem(), vmem(), hbm(), hbm(), hbm()],
        out_specs=(hbm(),) * (peers + 3),
        scratch_shapes=[
            pltpu.VMEM((rows, width), bf16),
            pltpu.VMEM((peers, rows, block), bf16),
            pltpu.VMEM((deep, across), bf16),
            pltpu.VMEM((2, deep // 2, across), bf16),
            dma((peers,)),
            dma((peers,)),
            dma,
            dma((2,)),
            dma,
        ],
        compiler_params=params(),
        cost_estimate=pl.CostEstimate(
            flops=6 * rows * width + 4 * deep * across,
            bytes_accessed=4 * rows * width + 4 * deep * across,
            transcendentals=0,
        ),
        name="front",
    )(place, gain, exponents, tokens, values, weight)


def update_kernel(place, own, other, base, momentum, new_params, new_momentum):
    step = pl.program_id(0)
    steps = pl.num_programs(0)

    def run(average):
        average = average.astype(f32)
        fresh = momentum_coef * momentum[...] + average
        new_momentum[...] = fresh
        new_params[...] = (
            base[...].astype(f32) - outer_rate * (average + momentum_coef * fresh)
        ).astype(bf16)

    @pl.when(step < steps // 2)
    def _():
        run(own[...])

    @pl.when(step >= steps // 2)
    def _():
        run(other[...])


def update(place, own, other, base, momentum):
    rows, width = base.shape
    steps = 4
    each = rows // steps
    near = steps // 2

    def row(i, place):
        return (lax.rem(i + place[2] * near, steps), 0)

    return pl.pallas_call(
        update_kernel,
        out_shape=(
            jax.ShapeDtypeStruct((rows, width), bf16),
            jax.ShapeDtypeStruct((rows, width), f32),
        ),
        grid_spec=pltpu.PrefetchScalarGridSpec(
            num_scalar_prefetch=1,
            grid=(steps,),
            in_specs=[
                pl.BlockSpec((each, width), lambda i, place: (jnp.minimum(i, near - 1), 0)),
                pl.BlockSpec((each, width), lambda i, place: (jnp.maximum(i - near, 0), 0)),
                pl.BlockSpec((each, width), row),
                pl.BlockSpec((each, width), row),
            ],
            out_specs=[pl.BlockSpec((each, width), row), pl.BlockSpec((each, width), row)],
        ),
        compiler_params=params(),
        cost_estimate=pl.CostEstimate(
            flops=8 * rows * width, bytes_accessed=14 * rows * width, transcendentals=0
        ),
        name="update",
    )(place, own, other, base, momentum)


def gather_group(value):
    group = lax.axis_size(GROUP)
    value = lax.all_to_all(
        jnp.broadcast_to(value, (group, *value.shape)), GROUP, 0, 0, tiled=True
    )
    return value.reshape(-1, value.shape[-1])


def scatter_group(value):
    group = lax.axis_size(GROUP)
    parts = value.reshape(group, value.shape[0] // group, value.shape[1])
    parts = lax.all_to_all(parts, GROUP, 0, 0, tiled=True)
    return jnp.sum(parts.astype(f32), axis=0)


def sum_thirds(value):
    third = lax.axis_size("zh")
    whole = lax.all_to_all(
        jnp.broadcast_to(value, (third, *value.shape)), "zh", 0, 0, tiled=True
    )
    return jnp.sum(whole, axis=0)


def project_kernel(*refs):
    ins, outs, scratch = refs[:7], refs[7:-7], refs[-7:]
    *blocks, mine, near, far = ins
    held, whole, first, rest, block_in, weight_in, out_sem = scratch
    half, quarter, width = mine.shape[1], near.shape[1], mine.shape[2]
    copies = []
    for i, (part, at, size) in enumerate(
        ((mine, 0, half), (near, half, quarter), (far, half + quarter, quarter))
    ):
        copies.append(
            pltpu.make_async_copy(part, whole.at[:, at : at + size, :], weight_in.at[i])
        )
    order = (*range(1, len(blocks)), 0)
    arrivals = {
        k: pltpu.make_async_copy(blocks[k], held.at[k], block_in.at[k]) for k in order
    }
    for copy in (*copies, *arrivals.values()):
        copy.start()
    for copy in copies:
        copy.wait()
    leaving = []
    for k in order:
        arrivals[k].wait()
        out = rest.at[k - 1] if k else first
        for kind in range(mine.shape[0]):
            out[:, kind * width : (kind + 1) * width] = jnp.dot(
                held[k], whole[kind], preferred_element_type=f32
            ).astype(out.dtype)
        leaving.append(pltpu.make_async_copy(out, outs[k], out_sem.at[k]))
        leaving[-1].start()
    for copy in leaving:
        copy.wait()


def project(tokens, weights):
    rows, depth = tokens[0].shape
    kinds, _, columns = weights[0].shape
    width = kinds * columns
    n = len(tokens)
    dma = pltpu.SemaphoreType.DMA
    return pl.pallas_call(
        project_kernel,
        out_shape=(jax.ShapeDtypeStruct((rows, width), f32),)
        + (jax.ShapeDtypeStruct((rows, width), bf16),) * (n - 1),
        in_specs=[hbm()] * (n + 3),
        out_specs=(hbm(),) * n,
        scratch_shapes=[
            pltpu.VMEM((n, rows, depth), bf16),
            pltpu.VMEM((kinds, depth, columns), bf16),
            pltpu.VMEM((rows, width), f32),
            pltpu.VMEM((n - 1, rows, width), bf16),
            dma((n,)),
            dma((3,)),
            dma((n,)),
        ],
        compiler_params=params(),
        cost_estimate=pl.CostEstimate(
            flops=2 * n * rows * depth * width,
            bytes_accessed=2 * depth * width + 2 * n * rows * depth + 4 * n * rows * width,
            transcendentals=0,
        ),
        name="project",
    )(*tokens, *weights)


def neighbour_share(share):
    yh, cores, yl = (lax.axis_size(a) for a in ("yh", "core", "yl"))
    ys = yh * yl
    moves = []
    for y in range(ys):
        for core in range(cores):
            to = (y + (1 if core == 0 else -1)) % ys
            moves.append(tuple((v // yl * cores + core) * yl + v % yl for v in (y, to)))
    return lax.ppermute(share, ("yh", "core", "yl"), moves)


def body(pseudo_grad, block_exponent, base_params, outer_momentum, tokens, norm_gain, kv_weight):
    x, yl, core = (lax.axis_index(a) for a in ("x", "yl", "core"))
    place = jnp.stack([x, yl, core]).astype(jnp.int32)
    after = lax.optimization_barrier

    *blocks, keep, send, share = front(
        place, tokens, norm_gain.reshape(1, -1), pseudo_grad[0], block_exponent[0].T, kv_weight
    )
    arrived = [blocks[0]] + [shift(block, "x", k) for k, block in enumerate(blocks) if k]
    near = neighbour_share(share)
    got = shift(send, "core", 1)

    pair = (keep.astype(f32) + got.astype(f32)).astype(bf16)
    total = scatter_group(pair)
    far = shift(near, "core", 1)
    average = (sum_thirds(total) / lax.axis_size(REPLICA)).astype(bf16)

    partial = project(arrived, (kv_weight, near, far))
    average, *partial = after((average, *partial))
    average = gather_group(average)
    other = shift(average, "core", 1)

    total = partial[0]
    for k, part in enumerate(partial):
        if k:
            total = total + shift(part, "x", -k).astype(f32)
    keys_values = total.astype(bf16)

    new_params, new_momentum = update(place, average, other, base_params, outer_momentum)
    return (new_params, new_momentum, keys_values)


def solution(mesh):
    cut = Mesh(mesh.devices.reshape(SHAPE), NAMES)
    placed = (
        P(REPLICA, FSDP, None),
        P(REPLICA, FSDP, None),
        P(FSDP, None),
        P(FSDP, None),
        P((*REPLICA, *FSDP), None),
        P(),
        P(None, FSDP, None),
    )
    return jax.shard_map(
        body,
        mesh=cut,
        in_specs=placed,
        out_specs=(P(FSDP, None), P(FSDP, None), P((*REPLICA, *FSDP), None)),
        check_vma=False,
    )
```

```python
import functools

import jax
import jax.numpy as jnp
from jax import lax
from jax.experimental import pallas as pl
from jax.experimental.pallas import tpu as pltpu
from jax.sharding import Mesh
from jax.sharding import PartitionSpec as P

outer_rate = 0.7
momentum_coef = 0.9
f32, bf16 = jnp.float32, jnp.bfloat16
VMEM_LIMIT = 48 * 1024 * 1024

SHAPE = (4, 3, 4, 2, 4, 2)
NAMES = ("yh", "zh", "zl", "core", "x", "yl")
REPLICA = ("yh", "zh", "zl", "core")
FSDP = ("x", "yl")
GROUP = ("yh", "zl")


def vmem():
    return pl.BlockSpec(memory_space=pltpu.VMEM)


def smem():
    return pl.BlockSpec(memory_space=pltpu.SMEM)


def params():
    return pltpu.CompilerParams(vmem_limit_bytes=VMEM_LIMIT)


def shift(value, axis, by):
    n = lax.axis_size(axis)
    return lax.ppermute(value, axis, [(i, (i + by) % n) for i in range(n)])


def hbm():
    return pl.BlockSpec(memory_space=pl.ANY)


def front_kernel(place, gain, exponents, tokens, values, *refs):
    (*blocks, keep, send), scratch = refs[: -len(FRONT)], refs[-len(FRONT) :]
    x, yl, core = place[0], place[1], place[2]
    held, normed, delta, dequantized, token_in, block_out, delta_in, delta_out = scratch
    peers, rows, block = normed.shape
    half = block // 2

    def chunk(i):
        at = pl.ds(i * block, block)
        return pltpu.make_async_copy(tokens.at[:, at], held.at[:, at], token_in.at[i])

    for i in range(peers):
        chunk(i).start()
    delta_copy = pltpu.make_async_copy(values, delta, delta_in)
    delta_copy.start()

    total = jnp.zeros((rows, 128), f32)
    for i in range(peers):
        chunk(i).wait()
        for at in range(i * block, (i + 1) * block, 128):
            piece = held[:, at : at + 128].astype(f32)
            total += piece * piece
    meansq = jnp.sum(total, axis=1, keepdims=True) / (peers * block)
    scale = lax.rsqrt(meansq + 1e-05)
    outs = []
    for k in (*range(1, peers), 0):
        first = lax.rem(x + k, peers) * block
        for at, part in ((0, yl), (half, 1 - yl)):
            columns = pl.ds(pl.multiple_of(first + part * half, half), half)
            piece = held[:, columns].astype(f32) * scale * gain[:, columns].astype(f32)
            normed[k, :, at : at + half] = piece.astype(bf16)
        outs.append(pltpu.make_async_copy(normed.at[k], blocks[k], block_out.at[k]))
        outs[-1].start()

    near, width = keep.shape
    count = exponents.shape[0]
    power = jnp.exp2(exponents[...].astype(f32))
    lane = lax.broadcasted_iota(jnp.int32, (count, width), 1)
    row = lax.broadcasted_iota(jnp.int32, (count, width), 0)
    spread = jnp.where(lane // (width // count) == row, 1.0, 0.0).astype(bf16)
    delta_copy.wait()
    for i, (out, part) in enumerate(((send, 1 - core), (keep, core))):
        start = pl.multiple_of(part * near, near)
        own = jnp.where(part == 0, power[:, :near], power[:, near:]).astype(bf16)
        wide = lax.dot_general(own, spread, (((0,), (0,)), ((), ())), preferred_element_type=f32)
        dequantized[i] = (delta[pl.ds(start, near), :].astype(f32) * wide).astype(bf16)
        outs.append(pltpu.make_async_copy(dequantized.at[i], out, delta_out.at[i]))
        outs[-1].start()
    for copy in outs:
        copy.wait()


FRONT = ("held", "normed", "delta", "dequantized", "in", "out", "din", "dout")


def front(place, tokens, gain, values, exponents):
    rows, width = tokens.shape
    peers = lax.axis_size("x")
    block = width // peers
    deep, across = values.shape
    dma = pltpu.SemaphoreType.DMA
    return pl.pallas_call(
        front_kernel,
        out_shape=(jax.ShapeDtypeStruct((rows, block), bf16),) * peers
        + (jax.ShapeDtypeStruct((deep // 2, across), bf16),) * 2,
        in_specs=[smem(), vmem(), vmem(), hbm(), hbm()],
        out_specs=(hbm(),) * (peers + 2),
        scratch_shapes=[
            pltpu.VMEM((rows, width), bf16),
            pltpu.VMEM((peers, rows, block), bf16),
            pltpu.VMEM((deep, across), bf16),
            pltpu.VMEM((2, deep // 2, across), bf16),
            dma((peers,)),
            dma((peers,)),
            dma,
            dma((2,)),
        ],
        compiler_params=params(),
        cost_estimate=pl.CostEstimate(
            flops=6 * rows * width + 4 * deep * across,
            bytes_accessed=4 * rows * width + 4 * deep * across,
            transcendentals=0,
        ),
        name="front",
    )(place, gain, exponents, tokens, values)


def update_kernel(place, own, other, base, momentum, new_params, new_momentum):
    step = pl.program_id(0)
    steps = pl.num_programs(0)

    def run(average):
        average = average.astype(f32)
        fresh = momentum_coef * momentum[...] + average
        new_momentum[...] = fresh
        new_params[...] = (
            base[...].astype(f32) - outer_rate * (average + momentum_coef * fresh)
        ).astype(bf16)

    @pl.when(step < steps // 2)
    def _():
        run(own[...])

    @pl.when(step >= steps // 2)
    def _():
        run(other[...])


def update(place, own, other, base, momentum):
    rows, width = base.shape
    steps = 4
    each = rows // steps
    near = steps // 2

    def row(i, place):
        return (lax.rem(i + place[2] * near, steps), 0)

    return pl.pallas_call(
        update_kernel,
        out_shape=(
            jax.ShapeDtypeStruct((rows, width), bf16),
            jax.ShapeDtypeStruct((rows, width), f32),
        ),
        grid_spec=pltpu.PrefetchScalarGridSpec(
            num_scalar_prefetch=1,
            grid=(steps,),
            in_specs=[
                pl.BlockSpec((each, width), lambda i, place: (jnp.minimum(i, near - 1), 0)),
                pl.BlockSpec((each, width), lambda i, place: (jnp.maximum(i - near, 0), 0)),
                pl.BlockSpec((each, width), row),
                pl.BlockSpec((each, width), row),
            ],
            out_specs=[pl.BlockSpec((each, width), row), pl.BlockSpec((each, width), row)],
        ),
        compiler_params=params(),
        cost_estimate=pl.CostEstimate(
            flops=8 * rows * width, bytes_accessed=14 * rows * width, transcendentals=0
        ),
        name="update",
    )(place, own, other, base, momentum)


def gather_group(value):
    group = lax.axis_size(GROUP)
    value = lax.all_to_all(
        jnp.broadcast_to(value, (group, *value.shape)), GROUP, 0, 0, tiled=True
    )
    return value.reshape(-1, value.shape[-1])


def scatter_group(value):
    group = lax.axis_size(GROUP)
    parts = value.reshape(group, value.shape[0] // group, value.shape[1])
    parts = lax.all_to_all(parts, GROUP, 0, 0, tiled=True)
    return jnp.sum(parts.astype(f32), axis=0)


def sum_thirds(value):
    third = lax.axis_size("zh")
    whole = lax.all_to_all(
        jnp.broadcast_to(value, (third, *value.shape)), "zh", 0, 0, tiled=True
    )
    return jnp.sum(whole, axis=0)


def project_kernel(*refs):
    ins, outs, scratch = refs[:6], refs[6:-7], refs[-7:]
    *blocks, mine, other = ins
    held, whole, first, rest, block_in, weight_in, out_sem = scratch
    half, width = mine.shape[1], mine.shape[2]
    copies = []
    for i, part in enumerate((mine, other)):
        rows = whole.at[:, i * half : (i + 1) * half, :]
        copies.append(pltpu.make_async_copy(part, rows, weight_in.at[i]))
    order = (*range(1, len(blocks)), 0)
    arrivals = {
        k: pltpu.make_async_copy(blocks[k], held.at[k], block_in.at[k]) for k in order
    }
    for copy in (*copies, *arrivals.values()):
        copy.start()
    for copy in copies:
        copy.wait()
    leaving = []
    for k in order:
        arrivals[k].wait()
        out = rest.at[k - 1] if k else first
        for kind in range(mine.shape[0]):
            out[:, kind * width : (kind + 1) * width] = jnp.dot(
                held[k], whole[kind], preferred_element_type=f32
            ).astype(out.dtype)
        leaving.append(pltpu.make_async_copy(out, outs[k], out_sem.at[k]))
        leaving[-1].start()
    for copy in leaving:
        copy.wait()


def project(tokens, weights):
    rows, depth = tokens[0].shape
    kinds, _, columns = weights[0].shape
    width = kinds * columns
    n = len(tokens)
    dma = pltpu.SemaphoreType.DMA
    return pl.pallas_call(
        project_kernel,
        out_shape=(jax.ShapeDtypeStruct((rows, width), f32),)
        + (jax.ShapeDtypeStruct((rows, width), bf16),) * (n - 1),
        in_specs=[hbm()] * (n + 2),
        out_specs=(hbm(),) * n,
        scratch_shapes=[
            pltpu.VMEM((n, rows, depth), bf16),
            pltpu.VMEM((kinds, depth, columns), bf16),
            pltpu.VMEM((rows, width), f32),
            pltpu.VMEM((n - 1, rows, width), bf16),
            dma((n,)),
            dma((2,)),
            dma((n,)),
        ],
        compiler_params=params(),
        cost_estimate=pl.CostEstimate(
            flops=2 * n * rows * depth * width,
            bytes_accessed=2 * depth * width + 2 * n * rows * depth + 4 * n * rows * width,
            transcendentals=0,
        ),
        name="project",
    )(*tokens, *weights)


def neighbour_weights(weight):
    yh, cores, yl = (lax.axis_size(a) for a in ("yh", "core", "yl"))
    ys = yh * yl
    moves = []
    for y in range(ys):
        for core in range(cores):
            to = (y + (1 if core == 0 else -1)) % ys
            moves.append(tuple((v // yl * cores + core) * yl + v % yl for v in (y, to)))
    return lax.ppermute(weight, ("yh", "core", "yl"), moves)


def body(pseudo_grad, block_exponent, base_params, outer_momentum, tokens, norm_gain, kv_weight):
    x, yl, core = (lax.axis_index(a) for a in ("x", "yl", "core"))
    place = jnp.stack([x, yl, core]).astype(jnp.int32)
    after = lax.optimization_barrier

    *blocks, keep, send = front(
        place, tokens, norm_gain.reshape(1, -1), pseudo_grad[0], block_exponent[0].T
    )
    arrived = [blocks[0]] + [shift(block, "x", k) for k, block in enumerate(blocks) if k]
    near = neighbour_weights(kv_weight)
    got = shift(send, "core", 1)

    pair = (keep.astype(f32) + got.astype(f32)).astype(bf16)
    total = scatter_group(pair)
    average = (sum_thirds(total) / lax.axis_size(REPLICA)).astype(bf16)

    partial = project(arrived, (kv_weight, near))
    average, *partial = after((average, *partial))
    average = gather_group(average)
    other = shift(average, "core", 1)

    total = partial[0]
    for k, part in enumerate(partial):
        if k:
            total = total + shift(part, "x", -k).astype(f32)
    keys_values = total.astype(bf16)

    new_params, new_momentum = update(place, average, other, base_params, outer_momentum)
    return (new_params, new_momentum, keys_values)


def solution(mesh):
    cut = Mesh(mesh.devices.reshape(SHAPE), NAMES)
    placed = (
        P(REPLICA, FSDP, None),
        P(REPLICA, FSDP, None),
        P(FSDP, None),
        P(FSDP, None),
        P((*REPLICA, *FSDP), None),
        P(),
        P(None, FSDP, None),
    )
    return jax.shard_map(
        body,
        mesh=cut,
        in_specs=placed,
        out_specs=(P(FSDP, None), P(FSDP, None), P((*REPLICA, *FSDP), None)),
        check_vma=False,
    )
```

```python
import functools

import jax
import jax.numpy as jnp
from jax import lax
from jax.experimental import pallas as pl
from jax.experimental.pallas import tpu as pltpu
from jax.sharding import Mesh
from jax.sharding import PartitionSpec as P

outer_rate = 0.7
momentum_coef = 0.9
f32, bf16 = jnp.float32, jnp.bfloat16
LANES = 128
MIB = 1024 * 1024

SHAPE = (4, 3, 4, 2, 4, 2)
NAMES = ("yh", "zh", "zl", "core", "x", "yl")
REPLICA = ("yh", "zh", "zl", "core")
FSDP = ("x", "yl")
GROUP = ("yh", "zl")


def vmem():
    return pl.BlockSpec(memory_space=pltpu.VMEM)


def smem():
    return pl.BlockSpec(memory_space=pltpu.SMEM)


def params(mib=48):
    return pltpu.CompilerParams(vmem_limit_bytes=mib * MIB)


def shift(value, axis, by):
    n = lax.axis_size(axis)
    return lax.ppermute(value, axis, [(i, (i + by) % n) for i in range(n)])


def hbm():
    return pl.BlockSpec(memory_space=pl.ANY)


def front_kernel(place, gain, exponents, tokens, values, *refs):
    (*blocks, keep, send), scratch = refs[: -len(FRONT)], refs[-len(FRONT) :]
    x, yl, core = place[0], place[1], place[2]
    held, normed, wide_gain, delta, dequantized = scratch[:5]
    token_in, block_out, delta_in, delta_out = scratch[5:]
    peers, rows, block = normed.shape
    half = block // 2

    def chunk(i):
        at = pl.ds(i * block, block)
        return pltpu.make_async_copy(tokens.at[:, at], held.at[:, at], token_in.at[i])

    for i in range(peers):
        chunk(i).start()
    delta_copy = pltpu.make_async_copy(values, delta, delta_in)
    delta_copy.start()

    wide_gain[...] = gain[...].astype(f32)

    total = jnp.zeros((rows, 128), f32)
    for i in range(peers):
        chunk(i).wait()
        for at in range(i * block, (i + 1) * block, 128):
            piece = held[:, at : at + 128].astype(f32)
            total += piece * piece
    meansq = jnp.sum(total, axis=1, keepdims=True) / (peers * block)
    scale = lax.rsqrt(meansq + 1e-05)
    outs = []
    for k in (*range(1, peers), 0):
        first = lax.rem(x + k, peers) * block
        for at, part in ((0, yl), (half, 1 - yl)):
            for inner in range(0, half, LANES):
                column = pl.multiple_of(first + part * half + inner, LANES)
                piece = held[:, pl.ds(column, LANES)].astype(f32) * scale
                piece = piece * wide_gain[pl.ds(column // LANES, 1), :]
                normed[k, :, at + inner : at + inner + LANES] = piece.astype(bf16)
        outs.append(pltpu.make_async_copy(normed.at[k], blocks[k], block_out.at[k]))
        outs[-1].start()

    near, width = keep.shape
    count = exponents.shape[0]
    power = jnp.exp2(exponents[...].astype(f32))
    lane = lax.broadcasted_iota(jnp.int32, (count, width), 1)
    row = lax.broadcasted_iota(jnp.int32, (count, width), 0)
    spread = jnp.where(lane // (width // count) == row, 1.0, 0.0).astype(bf16)
    delta_copy.wait()
    for i, (out, part) in enumerate(((send, 1 - core), (keep, core))):
        start = pl.multiple_of(part * near, near)
        own = jnp.where(part == 0, power[:, :near], power[:, near:]).astype(bf16)
        wide = lax.dot_general(own, spread, (((0,), (0,)), ((), ())), preferred_element_type=f32)
        dequantized[i] = (delta[pl.ds(start, near), :].astype(f32) * wide).astype(bf16)
        outs.append(pltpu.make_async_copy(dequantized.at[i], out, delta_out.at[i]))
        outs[-1].start()
    for copy in outs:
        copy.wait()


FRONT = ("held", "normed", "gain", "delta", "dequantized", "in", "out", "din", "dout")


def front(place, tokens, gain, values, exponents):
    rows, width = tokens.shape
    peers = lax.axis_size("x")
    block = width // peers
    deep, across = values.shape
    dma = pltpu.SemaphoreType.DMA
    return pl.pallas_call(
        front_kernel,
        out_shape=(jax.ShapeDtypeStruct((rows, block), bf16),) * peers
        + (jax.ShapeDtypeStruct((deep // 2, across), bf16),) * 2,
        in_specs=[smem(), vmem(), vmem(), hbm(), hbm()],
        out_specs=(hbm(),) * (peers + 2),
        scratch_shapes=[
            pltpu.VMEM((rows, width), bf16),
            pltpu.VMEM((peers, rows, block), bf16),
            pltpu.VMEM(gain.shape, f32),
            pltpu.VMEM((deep, across), bf16),
            pltpu.VMEM((2, deep // 2, across), bf16),
            dma((peers,)),
            dma((peers,)),
            dma,
            dma((2,)),
        ],
        compiler_params=params(60),
        cost_estimate=pl.CostEstimate(
            flops=6 * rows * width + 4 * deep * across,
            bytes_accessed=4 * rows * width + 4 * deep * across,
            transcendentals=0,
        ),
        name="front",
    )(place, gain, exponents, tokens, values)


def update_kernel(place, own, other, base, momentum, new_params, new_momentum):
    step = pl.program_id(0)
    steps = pl.num_programs(0)

    def run(average):
        average = average.astype(f32)
        fresh = momentum_coef * momentum[...] + average
        new_momentum[...] = fresh
        new_params[...] = (
            base[...].astype(f32) - outer_rate * (average + momentum_coef * fresh)
        ).astype(bf16)

    @pl.when(step < steps // 2)
    def _():
        run(own[...])

    @pl.when(step >= steps // 2)
    def _():
        run(other[...])


def update(place, own, other, base, momentum):
    rows, width = base.shape
    steps = 4
    each = rows // steps
    near = steps // 2

    def row(i, place):
        return (lax.rem(i + place[2] * near, steps), 0)

    return pl.pallas_call(
        update_kernel,
        out_shape=(
            jax.ShapeDtypeStruct((rows, width), bf16),
            jax.ShapeDtypeStruct((rows, width), f32),
        ),
        grid_spec=pltpu.PrefetchScalarGridSpec(
            num_scalar_prefetch=1,
            grid=(steps,),
            in_specs=[
                pl.BlockSpec((each, width), lambda i, place: (jnp.minimum(i, near - 1), 0)),
                pl.BlockSpec((each, width), lambda i, place: (jnp.maximum(i - near, 0), 0)),
                pl.BlockSpec((each, width), row),
                pl.BlockSpec((each, width), row),
            ],
            out_specs=[pl.BlockSpec((each, width), row), pl.BlockSpec((each, width), row)],
        ),
        compiler_params=params(),
        cost_estimate=pl.CostEstimate(
            flops=8 * rows * width, bytes_accessed=14 * rows * width, transcendentals=0
        ),
        name="update",
    )(place, own, other, base, momentum)


def gather_group(value):
    group = lax.axis_size(GROUP)
    value = lax.all_to_all(
        jnp.broadcast_to(value, (group, *value.shape)), GROUP, 0, 0, tiled=True
    )
    return value.reshape(-1, value.shape[-1])


def scatter_group(value):
    group = lax.axis_size(GROUP)
    parts = value.reshape(group, value.shape[0] // group, value.shape[1])
    parts = lax.all_to_all(parts, GROUP, 0, 0, tiled=True)
    return jnp.sum(parts.astype(f32), axis=0)


def sum_thirds(value):
    third = lax.axis_size("zh")
    whole = lax.all_to_all(
        jnp.broadcast_to(value, (third, *value.shape)), "zh", 0, 0, tiled=True
    )
    return jnp.sum(whole, axis=0)


def project_kernel(*refs):
    ins, outs, scratch = refs[:6], refs[6:-7], refs[-7:]
    *blocks, mine, other = ins
    held, whole, first, rest, block_in, weight_in, out_sem = scratch
    half, width = mine.shape[1], mine.shape[2]
    copies = []
    for i, part in enumerate((mine, other)):
        rows = whole.at[:, i * half : (i + 1) * half, :]
        copies.append(pltpu.make_async_copy(part, rows, weight_in.at[i]))
    order = (*range(1, len(blocks)), 0)
    arrivals = {
        k: pltpu.make_async_copy(blocks[k], held.at[k], block_in.at[k]) for k in order
    }
    for copy in (*copies, *arrivals.values()):
        copy.start()
    for copy in copies:
        copy.wait()
    leaving = []
    for k in order:
        arrivals[k].wait()
        out = rest.at[k - 1] if k else first
        for kind in range(mine.shape[0]):
            out[:, kind * width : (kind + 1) * width] = jnp.dot(
                held[k], whole[kind], preferred_element_type=f32
            ).astype(out.dtype)
        leaving.append(pltpu.make_async_copy(out, outs[k], out_sem.at[k]))
        leaving[-1].start()
    for copy in leaving:
        copy.wait()


def project(tokens, weights):
    rows, depth = tokens[0].shape
    kinds, _, columns = weights[0].shape
    width = kinds * columns
    n = len(tokens)
    dma = pltpu.SemaphoreType.DMA
    return pl.pallas_call(
        project_kernel,
        out_shape=(jax.ShapeDtypeStruct((rows, width), f32),)
        + (jax.ShapeDtypeStruct((rows, width), bf16),) * (n - 1),
        in_specs=[hbm()] * (n + 2),
        out_specs=(hbm(),) * n,
        scratch_shapes=[
            pltpu.VMEM((n, rows, depth), bf16),
            pltpu.VMEM((kinds, depth, columns), bf16),
            pltpu.VMEM((rows, width), f32),
            pltpu.VMEM((n - 1, rows, width), bf16),
            dma((n,)),
            dma((2,)),
            dma((n,)),
        ],
        compiler_params=params(),
        cost_estimate=pl.CostEstimate(
            flops=2 * n * rows * depth * width,
            bytes_accessed=2 * depth * width + 2 * n * rows * depth + 4 * n * rows * width,
            transcendentals=0,
        ),
        name="project",
    )(*tokens, *weights)


def neighbour_weights(weight):
    yh, cores, yl = (lax.axis_size(a) for a in ("yh", "core", "yl"))
    ys = yh * yl
    moves = []
    for y in range(ys):
        for core in range(cores):
            to = (y + (1 if core == 0 else -1)) % ys
            moves.append(tuple((v // yl * cores + core) * yl + v % yl for v in (y, to)))
    return lax.ppermute(weight, ("yh", "core", "yl"), moves)


def body(pseudo_grad, block_exponent, base_params, outer_momentum, tokens, norm_gain, kv_weight):
    x, yl, core = (lax.axis_index(a) for a in ("x", "yl", "core"))
    place = jnp.stack([x, yl, core]).astype(jnp.int32)
    after = lax.optimization_barrier

    *blocks, keep, send = front(
        place, tokens, norm_gain.reshape(-1, LANES), pseudo_grad[0], block_exponent[0].T
    )
    arrived = [blocks[0]] + [shift(block, "x", k) for k, block in enumerate(blocks) if k]
    near = neighbour_weights(kv_weight)
    got = shift(send, "core", 1)

    pair = (keep.astype(f32) + got.astype(f32)).astype(bf16)
    total = scatter_group(pair)
    average = (sum_thirds(total) / lax.axis_size(REPLICA)).astype(bf16)

    partial = project(arrived, (kv_weight, near))
    average, *partial = after((average, *partial))
    average = gather_group(average)
    other = shift(average, "core", 1)

    total = partial[0]
    for k, part in enumerate(partial):
        if k:
            total = total + shift(part, "x", -k).astype(f32)
    keys_values = total.astype(bf16)

    new_params, new_momentum = update(place, average, other, base_params, outer_momentum)
    return (new_params, new_momentum, keys_values)


def solution(mesh):
    cut = Mesh(mesh.devices.reshape(SHAPE), NAMES)
    placed = (
        P(REPLICA, FSDP, None),
        P(REPLICA, FSDP, None),
        P(FSDP, None),
        P(FSDP, None),
        P((*REPLICA, *FSDP), None),
        P(),
        P(None, FSDP, None),
    )
    return jax.shard_map(
        body,
        mesh=cut,
        in_specs=placed,
        out_specs=(P(FSDP, None), P(FSDP, None), P((*REPLICA, *FSDP), None)),
        check_vma=False,
    )
```
